32 devices in a mesh: row: 8 (over z, x), col: 4 (over y, core).
Axes of the slice: x: 2, y: 2, z: 4, core: 2. Of those that a mesh axis runs over, the one named last changes fastest.
Arguments:
- features: bfloat16 [4096, 1024], P(('col', 'row')), may hold values from -6 to 6
- weight: bfloat16 [1024, 1024], P('col'), may hold values from -0.1875 to 0.1875
- tile_values: bfloat16 [8, 4, 4, 8, 128, 128], P('row', 'col'), may hold values from -0.125 to 0.125
- block_cols: int32 [8, 4, 4, 8], P('row', 'col'), may hold values from 0 to 7, as said below
- tile_counts: int32 [8, 4, 4], P('row', 'col'), may hold values from 1 to 8, as said below
Outputs:
- hidden_out: bfloat16 [4096, 1024], P(('row', 'col'))
The draws below stay inside these ranges and needn't reach their ends.
Inputs may be any that keep to these rules, and one draw needn't show every extreme that they name: `block_cols`: the 8 entries of one block row of a tile are distinct block columns; values and block columns of slots that are not live are arbitrary. `tile_counts`: every tile has a block row with all 8 slots live.
All inputs are finite; a program needn't handle non-finite values.
Results may differ from the reference program's by a relative error of at most 0.019.
Values may be sent and summed in bfloat16 or wider, within the bound.
A program may use at most 64 MiB of HBM per device.

```python
import jax
import jax.numpy as jnp
from jax import lax

FEAT = 1024
BS = 128
SLOTS = 8
ROW_BLK = 4
COL_BLK = 8
NODES = 4096
N_ROW = 8
N_COL = 4


def draw_block_cols(key, part):
    scores = jax.random.randint(key, (N_ROW, N_COL, ROW_BLK, COL_BLK), 0, 2 ** 20, dtype=jnp.int32)
    scores = scores * COL_BLK + jnp.arange(COL_BLK, dtype=jnp.int32)
    order = jnp.argsort(scores, axis=-1, stable=True)
    return order[..., :SLOTS].astype(jnp.int32)


def draw_tile_counts(key, part):
    base_key = jax.random.fold_in(key, 11)
    floor_key = jax.random.fold_in(key, 23)
    where_key = jax.random.fold_in(key, 37)
    base = jax.random.randint(base_key, (N_ROW, N_COL, ROW_BLK), 1, SLOTS + 1, dtype=jnp.int32)
    floor_level = jax.random.randint(floor_key, (N_ROW, N_COL, 1), 1, SLOTS + 1, dtype=jnp.int32)
    counts = jnp.maximum(base, floor_level)
    full_row = jax.random.randint(where_key, (N_ROW, N_COL, 1), 0, ROW_BLK, dtype=jnp.int32)
    positions = jnp.arange(ROW_BLK, dtype=jnp.int32)[None, None, :]
    return jnp.where(positions == full_row, SLOTS, counts).astype(jnp.int32)


def shard_levels(rng, dims, cuts, least, high):
    level, own = 1.0, jax.random.fold_in(rng, 6)
    for position, shards_of in cuts:
        draws = jnp.exp(jax.random.uniform(jax.random.fold_in(own, position), (shards_of,), jnp.float32, least / len(cuts), high / len(cuts)))
        level = level * jnp.repeat(draws, dims[position] // shards_of).reshape([-1 if axis == position else 1 for axis in range(len(dims))])
    return level


def noise(own_key, extent, deviation, most, pieces=(), kind=jnp.bfloat16):
    array = deviation * jax.random.normal(own_key, extent, jnp.float32)
    if pieces:
        array = array * shard_levels(own_key, extent, pieces, -0.22, 0.18)
    return jnp.clip(array, -most, most).astype(kind)


def setup_inputs(seed: int = 0) -> dict:
    streams_of = jax.random.split(jax.random.key(seed), 6)
    features = noise(streams_of[0], (NODES, FEAT), 1.0, 6.0, ((0, 32),))
    weight = noise(streams_of[1], (FEAT, FEAT), FEAT ** -0.5, 0.1875, ((0, 4),))
    tile_values = noise(streams_of[2], (N_ROW, N_COL, ROW_BLK, SLOTS, BS, BS), (BS * SLOTS * N_COL // 2) ** -0.5, 0.125, ((0, 8), (1, 4)))
    block_cols = draw_block_cols(jax.random.fold_in(streams_of[5], 71), 0)
    tile_counts = draw_tile_counts(jax.random.fold_in(streams_of[5], 71), 0)
    return {"features": features, "weight": weight, "tile_values": tile_values, "block_cols": block_cols, "tile_counts": tile_counts}


def tile_term(slot_values, slot_cols, slot_count, column_rows):
    slot_total = slot_values.shape[1]
    block_size = slot_values.shape[-1]
    by_block = column_rows.reshape(-1, block_size, column_rows.shape[-1])
    gathered = by_block[slot_cols]
    live_slots = jnp.arange(slot_total, dtype=jnp.int32)[None, :] < slot_count[:, None]
    masked = jnp.where(live_slots[:, :, None, None], slot_values, jnp.zeros_like(slot_values))
    product = jnp.einsum('rsab,rsbf->raf', masked.astype(jnp.float32), gathered.astype(jnp.float32))
    return product.reshape(-1, product.shape[-1])


def reference(features, weight, tile_values, block_cols, tile_counts):
    panel_rows = COL_BLK * BS

    def one_panel(row_args):
        values_row, cols_row, counts_row = row_args

        def add_tile(running, tile_args):
            values_tile, cols_tile, counts_tile, column = tile_args
            column_rows = lax.dynamic_slice_in_dim(features, column * panel_rows, panel_rows, 0)
            rounded = tile_term(values_tile, cols_tile, counts_tile, column_rows).astype(jnp.bfloat16)
            rounded = lax.optimization_barrier(rounded)
            return running + rounded.astype(jnp.float32), None

        start_sum = jnp.zeros((ROW_BLK * BS, FEAT), jnp.float32)
        columns = jnp.arange(N_COL, dtype=jnp.int32)
        summed, unused = lax.scan(add_tile, start_sum, (values_row, cols_row, counts_row, columns))
        return summed.astype(jnp.bfloat16)

    aggregated = lax.map(one_panel, (tile_values, block_cols, tile_counts)).reshape(NODES, FEAT)
    product = jnp.dot(aggregated, weight, preferred_element_type=jnp.float32)
    return jnp.maximum(product, 0.0).astype(jnp.bfloat16)
```

```python
import functools

import jax
import jax.numpy as jnp
from jax import lax
from jax.experimental import pallas as pl
from jax.experimental.pallas import tpu as pltpu
from jax.sharding import PartitionSpec as P

MESH = pl.DeviceIdType.MESH
CHUNKS = 4


def kernel(rows_n, cols_n, x_n, cols_ref, counts_ref, feat_ref, weight_ref, vals_ref, out_ref,
           gath, wfull, vals, dense, psend, psib, ssum, ssend, srecv, acc,
           local_sem, zsend_sem, xsend_sem, grecv_sem, wsend_sem, wfwd_sem, wrecv_sem,
           psend_sem, precv_sem, ssend_sem, srecv_sem):
    z_n = rows_n // x_n
    q_n = cols_n // 2
    row = lax.axis_index("row")
    col = lax.axis_index("col")
    z, x = row // x_n, row % x_n
    q, core = col // 2, col % 2
    other = 1 - core
    sib = q * 2 + other
    row_blk, slots, bs = vals.shape[0], vals.shape[1], vals.shape[2]
    col_blk = rows_n
    out_rows = feat_ref.shape[0]
    feat = feat_ref.shape[1]
    fc = feat // CHUNKS
    wr = weight_ref.shape[0]

    z_steps = sorted(range(1, z_n), key=lambda d: min(d, z_n - d))
    z_to = [((z + d) % z_n) * x_n + x for d in z_steps]
    z_from = [((z + z_n - d) % z_n) * x_n + x for d in z_steps]
    x_steps = list(range(1, x_n))
    q_steps = list(range(1, q_n))
    q_to = [((q + d) % q_n) for d in q_steps]
    q_from = [((q + q_n - d) % q_n) for d in q_steps]

    local = [
        pltpu.make_async_copy(vals_ref.at[0, 0], vals, local_sem.at[0]),
        pltpu.make_async_copy(weight_ref, wfull.at[pl.ds(pl.multiple_of(col * wr, wr), wr)], local_sem.at[1]),
    ]
    for c in range(CHUNKS):
        local.append(pltpu.make_async_copy(
            feat_ref.at[:, pl.ds(c * fc, fc)], gath.at[c, row], local_sem.at[2 + c]))
    for copy in local:
        copy.start()

    barrier = pltpu.get_barrier_semaphore()
    peers = 0
    for r in z_to + [z * x_n + (x + d) % x_n for d in x_steps]:
        pl.semaphore_signal(barrier, inc=1, device_id={"row": r, "col": col}, device_id_type=MESH)
        peers += 1
    for j in [t * 2 + core for t in q_to] + [sib]:
        pl.semaphore_signal(barrier, inc=1, device_id={"row": row, "col": j}, device_id_type=MESH)
        peers += 1
    pl.semaphore_wait(barrier, peers)

    sends = []

    def send(src, dst, ssem, rsem, r, j):
        copy = pltpu.make_async_remote_copy(
            src_ref=src, dst_ref=dst, send_sem=ssem, recv_sem=rsem,
            device_id={"row": r, "col": j}, device_id_type=MESH)
        copy.start()
        sends.append(copy)

    def arrived(ref, sem):
        pltpu.make_async_copy(ref, ref, sem).wait()

    def x_send(c, origin, n, src):
        for k, d in enumerate(x_steps):
            send(src, gath.at[c, origin], xsend_sem.at[c, n, k], grecv_sem.at[c, origin],
                 z * x_n + (x + d) % x_n, col)

    for c in range(CHUNKS):
        src = feat_ref.at[:, pl.ds(c * fc, fc)]
        for k, r in enumerate(z_to):
            send(src, gath.at[c, row], zsend_sem.at[c, k], grecv_sem.at[c, row], r, col)
        x_send(c, row, 0, src)

    wmine = pl.ds(pl.multiple_of(col * wr, wr), wr)
    for k, t in enumerate(q_to):
        send(weight_ref, wfull.at[wmine], wsend_sem.at[k], wrecv_sem.at[col], row, t * 2 + core)
    send(weight_ref, wfull.at[wmine], wfwd_sem.at[0], wrecv_sem.at[col], row, sib)

    local[0].wait()

    def make_dense(r, carry):
        count = counts_ref[0, 0, r]
        ids = [cols_ref[0, 0, r, s] for s in range(slots)]
        for c in range(col_blk):
            slot = jnp.int32(0)
            live = jnp.int32(0)
            for s in range(slots):
                hit = jnp.logical_and(ids[s] == c, s < count)
                slot = jnp.where(hit, s, slot)
                live = jnp.where(hit, 1, live)
            block = vals[r, slot]
            dense[r % 2, r // 2, :, c * bs:(c + 1) * bs] = jnp.where(live == 1, block, jnp.zeros_like(block))
        return carry

    lax.fori_loop(0, row_blk, make_dense, 0)

    def forward(c):
        for n, r in enumerate(z_from):
            arrived(gath.at[c, r], grecv_sem.at[c, r])
            x_send(c, r, n + 1, gath.at[c, r])

    def w_forward():
        for k, t in enumerate(q_from):
            part = pl.ds(pl.multiple_of((t * 2 + core) * wr, wr), wr)
            arrived(wfull.at[part], wrecv_sem.at[t * 2 + core])
            send(wfull.at[part], wfull.at[part], wfwd_sem.at[k + 1], wrecv_sem.at[t * 2 + core], row, sib)

    def w_arrive():
        local[1].wait()
        for t in range(q_n):
            j = t * 2 + other
            part = pl.ds(pl.multiple_of(j * wr, wr), wr)
            arrived(wfull.at[part], wrecv_sem.at[j])

    per = max(1, min(q_n, 256 // out_rows))

    def aggregate(c):
        local[2 + c].wait()
        for d in x_steps:
            for zz in range(z_n):
                r = zz * x_n + (x + d) % x_n
                arrived(gath.at[c, r], grecv_sem.at[c, r])

        def dots(which, put):
            def step(t, carry):
                a = dense[which, pl.ds(t * per, per)].reshape(per * out_rows, col_blk * bs)
                g = gath[c].reshape(col_blk * bs, fc)
                put(t, jnp.dot(a, g, preferred_element_type=jnp.float32).reshape(per, out_rows, fc))
                return carry
            if q_n == per:
                step(0, 0)
            else:
                lax.fori_loop(0, q_n // per, step, 0)

        def put_send(t, v):
            psend[c, pl.ds(t * per, per)] = v.astype(psend.dtype)

        def put_sum(t, v):
            ssum[c, pl.ds(t * per, per)] = v

        dots(other, put_send)
        send(psend.at[c], psib.at[c], psend_sem.at[c], precv_sem.at[c], row, sib)
        dots(core, put_sum)

    def pair_sum(c):
        arrived(psib.at[c], precv_sem.at[c])
        total = ssum[c] + psib[c].astype(jnp.float32)
        ssum[c] = total
        ssend[c] = total.astype(ssend.dtype)
        for k, t in enumerate(q_to):
            send(ssend.at[c, t], srecv.at[c, q], ssend_sem.at[c, k], srecv_sem.at[c, q], row, t * 2 + core)

    def finish(c):
        total = ssum[c, q]
        for t in q_from:
            arrived(srecv.at[c, t], srecv_sem.at[c, t])
            total = total + srecv[c, t].astype(jnp.float32)
        part = jnp.dot(total.astype(jnp.bfloat16), wfull[c * fc:(c + 1) * fc, :],
                       preferred_element_type=jnp.float32)
        if c == 0:
            acc[...] = part
        elif c < CHUNKS - 1:
            acc[...] += part
        else:
            out_ref[...] = jnp.maximum(acc[...] + part, 0.0).astype(out_ref.dtype)

    forward(0)
    for step in range(1, CHUNKS + 4):
        if step < CHUNKS:
            forward(step)
        if step == 2:
            w_forward()
        if 0 <= step - 1 < CHUNKS:
            aggregate(step - 1)
        if 0 <= step - 2 < CHUNKS:
            pair_sum(step - 2)
        if step == 3:
            w_arrive()
        if 0 <= step - 3 < CHUNKS:
            finish(step - 3)
    for copy in sends:
        copy.wait_send()


def solution(mesh):
    rows_n, cols_n = mesh.shape["row"], mesh.shape["col"]
    x_n = 1 << ((rows_n.bit_length() - 1) // 2)
    z_n = rows_n // x_n
    q_n = cols_n // 2

    def body(features, weight, tile_values, block_cols, tile_counts):
        out_rows, feat = features.shape
        _, _, row_blk, slots, bs, _ = tile_values.shape
        fc = feat // CHUNKS
        wide = weight.shape[1]
        dma = pltpu.SemaphoreType.DMA
        bf16, f32 = jnp.bfloat16, jnp.float32
        flops = 2 * row_blk * bs * rows_n * bs * feat + 2 * out_rows * feat * wide
        return pl.pallas_call(
            functools.partial(kernel, rows_n, cols_n, x_n),
            out_shape=jax.ShapeDtypeStruct((out_rows, wide), bf16),
            in_specs=[pl.BlockSpec(memory_space=pltpu.SMEM)] * 2 + [pl.BlockSpec(memory_space=pl.ANY)] * 3,
            out_specs=pl.BlockSpec(memory_space=pltpu.VMEM),
            scratch_shapes=[
                pltpu.VMEM((CHUNKS, rows_n, out_rows, fc), bf16),
                pltpu.VMEM((feat, wide), bf16),
                pltpu.VMEM((row_blk, slots, bs, bs), bf16),
                pltpu.VMEM((2, q_n, out_rows, rows_n * bs), bf16),
                pltpu.VMEM((CHUNKS, q_n, out_rows, fc), bf16),
                pltpu.VMEM((CHUNKS, q_n, out_rows, fc), bf16),
                pltpu.VMEM((CHUNKS, q_n, out_rows, fc), f32),
                pltpu.VMEM((CHUNKS, q_n, out_rows, fc), bf16),
                pltpu.VMEM((CHUNKS, q_n, out_rows, fc), bf16),
                pltpu.VMEM((out_rows, wide), f32),
                dma((2 + CHUNKS,)),
                dma((CHUNKS, max(1, z_n - 1))),
                dma((CHUNKS, z_n, max(1, x_n - 1))),
                dma((CHUNKS, rows_n)),
                dma((max(1, q_n - 1),)),
                dma((q_n,)),
                dma((cols_n,)),
                dma((CHUNKS,)),
                dma((CHUNKS,)),
                dma((CHUNKS, max(1, q_n - 1))),
                dma((CHUNKS, q_n)),
            ],
            compiler_params=pltpu.CompilerParams(
                collective_id=0, has_side_effects=True, vmem_limit_bytes=48 * 1024 * 1024),
            cost_estimate=pl.CostEstimate(flops=flops, bytes_accessed=4 * 1024 * 1024, transcendentals=0),
        )(block_cols, tile_counts, features, weight, tile_values)

    in_specs = (
        P(("col", "row"), None),
        P("col", None),
        P("row", "col", None, None, None, None),
        P("row", "col", None, None),
        P("row", "col", None),
    )
    return jax.shard_map(body, mesh=mesh, in_specs=in_specs, out_specs=P(("row", "col"), None), check_vma=False)
```

```python
import functools

import jax
import jax.numpy as jnp
from jax import lax
from jax.experimental import pallas as pl
from jax.experimental.pallas import tpu as pltpu
from jax.sharding import PartitionSpec as P

MESH = pl.DeviceIdType.MESH
CHUNKS = 4
AHEAD = 2
LATE = 1


def kernel(rows_n, cols_n, x_n, cols_ref, counts_ref, feat_ref, weight_ref, vals_ref, out_ref,
           gath, wfull, vals, dense, psend, psib, ssum, ssend, srecv, acc,
           local_sem, zsend_sem, xsend_sem, grecv_sem, wsend_sem, wfwd_sem, wrecv_sem,
           psend_sem, precv_sem, ssend_sem, srecv_sem):
    z_n = rows_n // x_n
    q_n = cols_n // 2
    row = lax.axis_index("row")
    col = lax.axis_index("col")
    z, x = row // x_n, row % x_n
    q, core = col // 2, col % 2
    other = 1 - core
    sib = q * 2 + other
    row_blk, slots, bs = vals.shape[0], vals.shape[1], vals.shape[2]
    col_blk = rows_n
    out_rows = feat_ref.shape[0]
    feat = feat_ref.shape[1]
    fc = feat // CHUNKS
    wr = weight_ref.shape[0]

    has_up, has_down = z < z_n - 1, z > 0
    up, down = (z + 1) * x_n + x, (z - 1) * x_n + x
    x_steps = list(range(1, x_n))
    q_steps = list(range(1, q_n))
    q_to = [((q + d) % q_n) for d in q_steps]
    q_from = [((q + q_n - d) % q_n) for d in q_steps]

    local = [
        pltpu.make_async_copy(vals_ref.at[0, 0], vals, local_sem.at[0]),
        pltpu.make_async_copy(weight_ref, wfull.at[pl.ds(pl.multiple_of(col * wr, wr), wr)], local_sem.at[1]),
    ]
    for c in range(CHUNKS):
        local.append(pltpu.make_async_copy(
            feat_ref.at[:, pl.ds(c * fc, fc)], gath.at[c, row], local_sem.at[2 + c]))
    for copy in local:
        copy.start()

    barrier = pltpu.get_barrier_semaphore()
    peers = jnp.where(has_up, 1, 0) + jnp.where(has_down, 1, 0)
    for present, r in ((has_up, up), (has_down, down)):
        @pl.when(present)
        def _():
            pl.semaphore_signal(barrier, inc=1, device_id={"row": r, "col": col}, device_id_type=MESH)
    for r in [z * x_n + (x + d) % x_n for d in x_steps]:
        pl.semaphore_signal(barrier, inc=1, device_id={"row": r, "col": col}, device_id_type=MESH)
        peers += 1
    for j in [t * 2 + core for t in q_to] + [sib]:
        pl.semaphore_signal(barrier, inc=1, device_id={"row": row, "col": j}, device_id_type=MESH)
        peers += 1
    pl.semaphore_wait(barrier, peers)

    sends = []

    def send(src, dst, ssem, rsem, r, j, present=None):
        copy = pltpu.make_async_remote_copy(
            src_ref=src, dst_ref=dst, send_sem=ssem, recv_sem=rsem,
            device_id={"row": r, "col": j}, device_id_type=MESH)
        if present is None:
            copy.start()
        else:
            pl.when(present)(copy.start)
        sends.append((copy, present))

    def arrived(ref, sem):
        pltpu.make_async_copy(ref, ref, sem).wait()

    def x_send(c, origin, n, src, present=None):
        for k, d in enumerate(x_steps):
            send(src, gath.at[c, origin], xsend_sem.at[c, n, k], grecv_sem.at[c, origin],
                 z * x_n + (x + d) % x_n, col, present)

    def own(c):
        src = feat_ref.at[:, pl.ds(c * fc, fc)]
        send(src, gath.at[c, row], zsend_sem.at[c, 0], grecv_sem.at[c, row], up, col, has_up)
        send(src, gath.at[c, row], zsend_sem.at[c, 1], grecv_sem.at[c, row], down, col, has_down)
        x_send(c, row, 0, src)

    for c in range(AHEAD):
        own(c)

    wmine = pl.ds(pl.multiple_of(col * wr, wr), wr)
    for k, t in enumerate(q_to):
        send(weight_ref, wfull.at[wmine], wsend_sem.at[k], wrecv_sem.at[col], row, t * 2 + core)
    send(weight_ref, wfull.at[wmine], wfwd_sem.at[0], wrecv_sem.at[col], row, sib)

    local[0].wait()

    def make_dense(r, carry):
        count = counts_ref[0, 0, r]
        ids = [cols_ref[0, 0, r, s] for s in range(slots)]
        for c in range(col_blk):
            slot = jnp.int32(0)
            live = jnp.int32(0)
            for s in range(slots):
                hit = jnp.logical_and(ids[s] == c, s < count)
                slot = jnp.where(hit, s, slot)
                live = jnp.where(hit, 1, live)
            block = vals[r, slot]
            dense[r % 2, r // 2, :, c * bs:(c + 1) * bs] = jnp.where(live == 1, block, jnp.zeros_like(block))
        return carry

    lax.fori_loop(0, row_blk, make_dense, 0)

    def forward(c):
        for d in range(1, z_n):
            for side in range(2):
                r = row - d * x_n if side == 0 else row + d * x_n
                here = z >= d if side == 0 else z + d < z_n
                there = jnp.logical_and(here, has_up if side == 0 else has_down)
                src = gath.at[c, r]
                n = 2 * d + side - 1
                pl.when(here)(functools.partial(arrived, src, grecv_sem.at[c, r]))
                send(src, src, zsend_sem.at[c, n + 1], grecv_sem.at[c, r], up if side == 0 else down, col, there)
                x_send(c, r, n, src, here)

    def w_forward():
        for k, t in enumerate(q_from):
            part = pl.ds(pl.multiple_of((t * 2 + core) * wr, wr), wr)
            arrived(wfull.at[part], wrecv_sem.at[t * 2 + core])
            send(wfull.at[part], wfull.at[part], wfwd_sem.at[k + 1], wrecv_sem.at[t * 2 + core], row, sib)

    def w_arrive():
        local[1].wait()
        for t in range(q_n):
            j = t * 2 + other
            part = pl.ds(pl.multiple_of(j * wr, wr), wr)
            arrived(wfull.at[part], wrecv_sem.at[j])

    per = max(1, min(q_n, 256 // out_rows))

    def aggregate(c):
        local[2 + c].wait()
        for d in x_steps:
            for zz in range(z_n):
                r = zz * x_n + (x + d) % x_n
                arrived(gath.at[c, r], grecv_sem.at[c, r])

        def dots(which, put):
            def step(t, carry):
                a = dense[which, pl.ds(t * per, per)].reshape(per * out_rows, col_blk * bs)
                g = gath[c].reshape(col_blk * bs, fc)
                put(t, jnp.dot(a, g, preferred_element_type=jnp.float32).reshape(per, out_rows, fc))
                return carry
            if q_n == per:
                step(0, 0)
            else:
                lax.fori_loop(0, q_n // per, step, 0)

        def put_send(t, v):
            psend[c, pl.ds(t * per, per)] = v.astype(psend.dtype)

        def put_sum(t, v):
            ssum[c, pl.ds(t * per, per)] = v

        dots(other, put_send)
        send(psend.at[c], psib.at[c], psend_sem.at[c], precv_sem.at[c], row, sib)
        dots(core, put_sum)

    def pair_sum(c):
        arrived(psib.at[c], precv_sem.at[c])
        total = ssum[c] + psib[c].astype(jnp.float32)
        ssum[c] = total
        ssend[c] = total.astype(ssend.dtype)
        for k, t in enumerate(q_to):
            send(ssend.at[c, t], srecv.at[c, q], ssend_sem.at[c, k], srecv_sem.at[c, q], row, t * 2 + core)

    def finish(c):
        total = ssum[c, q]
        for t in q_from:
            arrived(srecv.at[c, t], srecv_sem.at[c, t])
            total = total + srecv[c, t].astype(jnp.float32)
        part = jnp.dot(total.astype(jnp.bfloat16), wfull[c * fc:(c + 1) * fc, :],
                       preferred_element_type=jnp.float32)
        if c == 0:
            acc[...] = part
        elif c < CHUNKS - 1:
            acc[...] += part
        else:
            out_ref[...] = jnp.maximum(acc[...] + part, 0.0).astype(out_ref.dtype)

    for step in range(CHUNKS + LATE + 2):
        if step + AHEAD < CHUNKS:
            own(step + AHEAD)
        if step < CHUNKS:
            forward(step)
        if step == 1:
            w_forward()
        if 0 <= step - LATE < CHUNKS:
            aggregate(step - LATE)
        if 0 <= step - LATE - 1 < CHUNKS:
            pair_sum(step - LATE - 1)
        if step == LATE + 2:
            w_arrive()
        if 0 <= step - LATE - 2 < CHUNKS:
            finish(step - LATE - 2)
    for copy, present in sends:
        if present is None:
            copy.wait_send()
        else:
            pl.when(present)(copy.wait_send)


def solution(mesh):
    rows_n, cols_n = mesh.shape["row"], mesh.shape["col"]
    x_n = 1 << ((rows_n.bit_length() - 1) // 2)
    z_n = rows_n // x_n
    q_n = cols_n // 2

    def body(features, weight, tile_values, block_cols, tile_counts):
        out_rows, feat = features.shape
        _, _, row_blk, slots, bs, _ = tile_values.shape
        fc = feat // CHUNKS
        wide = weight.shape[1]
        dma = pltpu.SemaphoreType.DMA
        bf16, f32 = jnp.bfloat16, jnp.float32
        flops = 2 * row_blk * bs * rows_n * bs * feat + 2 * out_rows * feat * wide
        return pl.pallas_call(
            functools.partial(kernel, rows_n, cols_n, x_n),
            out_shape=jax.ShapeDtypeStruct((out_rows, wide), bf16),
            in_specs=[pl.BlockSpec(memory_space=pltpu.SMEM)] * 2 + [pl.BlockSpec(memory_space=pl.ANY)] * 3,
            out_specs=pl.BlockSpec(memory_space=pltpu.VMEM),
            scratch_shapes=[
                pltpu.VMEM((CHUNKS, rows_n, out_rows, fc), bf16),
                pltpu.VMEM((feat, wide), bf16),
                pltpu.VMEM((row_blk, slots, bs, bs), bf16),
                pltpu.VMEM((2, q_n, out_rows, rows_n * bs), bf16),
                pltpu.VMEM((CHUNKS, q_n, out_rows, fc), bf16),
                pltpu.VMEM((CHUNKS, q_n, out_rows, fc), bf16),
                pltpu.VMEM((CHUNKS, q_n, out_rows, fc), f32),
                pltpu.VMEM((CHUNKS, q_n, out_rows, fc), bf16),
                pltpu.VMEM((CHUNKS, q_n, out_rows, fc), bf16),
                pltpu.VMEM((out_rows, wide), f32),
                dma((2 + CHUNKS,)),
                dma((CHUNKS, 2 * z_n)),
                dma((CHUNKS, 2 * z_n, max(1, x_n - 1))),
                dma((CHUNKS, rows_n)),
                dma((max(1, q_n - 1),)),
                dma((q_n,)),
                dma((cols_n,)),
                dma((CHUNKS,)),
                dma((CHUNKS,)),
                dma((CHUNKS, max(1, q_n - 1))),
                dma((CHUNKS, q_n)),
            ],
            compiler_params=pltpu.CompilerParams(
                collective_id=0, has_side_effects=True, vmem_limit_bytes=63 * 1024 * 1024),
            cost_estimate=pl.CostEstimate(flops=flops, bytes_accessed=4 * 1024 * 1024, transcendentals=0),
        )(block_cols, tile_counts, features, weight, tile_values)

    in_specs = (
        P(("col", "row"), None),
        P("col", None),
        P("row", "col", None, None, None, None),
        P("row", "col", None, None),
        P("row", "col", None),
    )
    return jax.shard_map(body, mesh=mesh, in_specs=in_specs, out_specs=P(("row", "col"), None), check_vma=False)
```

```python
import functools

import jax
import jax.numpy as jnp
from jax import lax
from jax.experimental import pallas as pl
from jax.experimental.pallas import tpu as pltpu
from jax.sharding import PartitionSpec as P

MESH = pl.DeviceIdType.MESH
CHUNKS = 4
AHEAD = 4
LATE = 2
WFWD = 4


def kernel(rows_n, cols_n, x_n, cols_ref, counts_ref, feat_ref, weight_ref, vals_ref, out_ref,
           gath, wfull, vals, dense, psend, psib, ssum, ssend, srecv, acc,
           local_sem, zsend_sem, xsend_sem, grecv_sem, wsend_sem, wfwd_sem, wrecv_sem,
           psend_sem, precv_sem, ssend_sem, srecv_sem):
    z_n = rows_n // x_n
    q_n = cols_n // 2
    row = lax.axis_index("row")
    col = lax.axis_index("col")
    z, x = row // x_n, row % x_n
    q, core = col // 2, col % 2
    other = 1 - core
    sib = q * 2 + other
    row_blk, slots, bs = vals.shape[0], vals.shape[1], vals.shape[2]
    col_blk = rows_n
    out_rows = feat_ref.shape[0]
    feat = feat_ref.shape[1]
    fc = feat // CHUNKS
    wr = weight_ref.shape[0]
    wpart = weight_ref.shape[1] // CHUNKS

    has_up, has_down = z < z_n - 1, z > 0
    up, down = (z + 1) * x_n + x, (z - 1) * x_n + x
    x_steps = list(range(1, x_n))
    q_steps = list(range(1, q_n))
    q_to = [((q + d) % q_n) for d in q_steps]
    q_from = [((q + q_n - d) % q_n) for d in q_steps]

    local = [
        pltpu.make_async_copy(vals_ref.at[0, 0], vals, local_sem.at[0]),
        pltpu.make_async_copy(weight_ref, wfull.at[pl.ds(pl.multiple_of(col * wr, wr), wr)], local_sem.at[1]),
    ]
    for c in range(CHUNKS):
        local.append(pltpu.make_async_copy(
            feat_ref.at[:, pl.ds(c * fc, fc)], gath.at[c, row], local_sem.at[2 + c]))
    for copy in local:
        copy.start()

    barrier = pltpu.get_barrier_semaphore()
    peers = jnp.where(has_up, 1, 0) + jnp.where(has_down, 1, 0)
    for present, r in ((has_up, up), (has_down, down)):
        @pl.when(present)
        def _():
            pl.semaphore_signal(barrier, inc=1, device_id={"row": r, "col": col}, device_id_type=MESH)
    for r in [z * x_n + (x + d) % x_n for d in x_steps]:
        pl.semaphore_signal(barrier, inc=1, device_id={"row": r, "col": col}, device_id_type=MESH)
        peers += 1
    for j in [t * 2 + core for t in q_to] + [sib]:
        pl.semaphore_signal(barrier, inc=1, device_id={"row": row, "col": j}, device_id_type=MESH)
        peers += 1
    pl.semaphore_wait(barrier, peers)

    sends = []

    def send(src, dst, ssem, rsem, r, j, present=None):
        copy = pltpu.make_async_remote_copy(
            src_ref=src, dst_ref=dst, send_sem=ssem, recv_sem=rsem,
            device_id={"row": r, "col": j}, device_id_type=MESH)
        if present is None:
            copy.start()
        else:
            pl.when(present)(copy.start)
        sends.append((copy, present))

    def arrived(ref, sem):
        pltpu.make_async_copy(ref, ref, sem).wait()

    def x_send(c, origin, n, src, present=None):
        for k, d in enumerate(x_steps):
            send(src, gath.at[c, origin], xsend_sem.at[c, n, k], grecv_sem.at[c, origin],
                 z * x_n + (x + d) % x_n, col, present)

    def own(c):
        local[2 + c].wait()
        src = gath.at[c, row]
        send(src, gath.at[c, row], zsend_sem.at[c, 0], grecv_sem.at[c, row], up, col, has_up)
        send(src, gath.at[c, row], zsend_sem.at[c, 1], grecv_sem.at[c, row], down, col, has_down)
        x_send(c, row, 0, src)

    for c in range(AHEAD):
        own(c)

    def w_own(c):
        lane = pl.ds(c * wpart, wpart)
        mine = wfull.at[pl.ds(pl.multiple_of(col * wr, wr), wr), lane]
        for k, t in enumerate(q_to):
            send(weight_ref.at[:, lane], mine, wsend_sem.at[c, k], wrecv_sem.at[col], row, t * 2 + core)
        if c == CHUNKS - 1:
            mine = wfull.at[pl.ds(pl.multiple_of(col * wr, wr), wr)]
            send(weight_ref, mine, wfwd_sem.at[0], wrecv_sem.at[col], row, sib)

    local[0].wait()

    def make_dense(r, carry):
        count = counts_ref[0, 0, r]
        ids = [cols_ref[0, 0, r, s] for s in range(slots)]
        for c in range(col_blk):
            slot = jnp.int32(0)
            live = jnp.int32(0)
            for s in range(slots):
                hit = jnp.logical_and(ids[s] == c, s < count)
                slot = jnp.where(hit, s, slot)
                live = jnp.where(hit, 1, live)
            block = vals[r, slot]
            dense[r % 2, r // 2, :, c * bs:(c + 1) * bs] = jnp.where(live == 1, block, jnp.zeros_like(block))
        return carry

    lax.fori_loop(0, row_blk, make_dense, 0)

    def forward(c):
        for d in range(1, z_n):
            for side in range(2):
                r = row - d * x_n if side == 0 else row + d * x_n
                here = z >= d if side == 0 else z + d < z_n
                there = jnp.logical_and(here, has_up if side == 0 else has_down)
                src = gath.at[c, r]
                n = 2 * d + side - 1
                pl.when(here)(functools.partial(arrived, src, grecv_sem.at[c, r]))
                send(src, src, zsend_sem.at[c, n + 1], grecv_sem.at[c, r], up if side == 0 else down, col, there)
                x_send(c, r, n, src, here)

    def w_forward():
        for k, t in enumerate(q_from):
            part = pl.ds(pl.multiple_of((t * 2 + core) * wr, wr), wr)
            arrived(wfull.at[part], wrecv_sem.at[t * 2 + core])
            send(wfull.at[part], wfull.at[part], wfwd_sem.at[k + 1], wrecv_sem.at[t * 2 + core], row, sib)

    def w_arrive():
        local[1].wait()
        for t in range(q_n):
            j = t * 2 + other
            part = pl.ds(pl.multiple_of(j * wr, wr), wr)
            arrived(wfull.at[part], wrecv_sem.at[j])

    per = max(1, min(q_n, 256 // out_rows))

    def aggregate(c):
        for d in x_steps:
            for zz in range(z_n):
                r = zz * x_n + (x + d) % x_n
                arrived(gath.at[c, r], grecv_sem.at[c, r])

        def dots(which, put):
            def step(t, carry):
                a = dense[which, pl.ds(t * per, per)].reshape(per * out_rows, col_blk * bs)
                g = gath[c].reshape(col_blk * bs, fc)
                put(t, jnp.dot(a, g, preferred_element_type=jnp.float32).reshape(per, out_rows, fc))
                return carry
            if q_n == per:
                step(0, 0)
            else:
                lax.fori_loop(0, q_n // per, step, 0)

        def put_send(t, v):
            psend[c, pl.ds(t * per, per)] = v.astype(psend.dtype)

        def put_sum(t, v):
            ssum[c, pl.ds(t * per, per)] = v

        dots(other, put_send)
        send(psend.at[c], psib.at[c], psend_sem.at[c], precv_sem.at[c], row, sib)
        dots(core, put_sum)

    def pair_sum(c):
        arrived(psib.at[c], precv_sem.at[c])
        total = ssum[c] + psib[c].astype(jnp.float32)
        ssum[c] = total
        ssend[c] = total.astype(ssend.dtype)
        for k, t in enumerate(q_to):
            send(ssend.at[c, t], srecv.at[c, q], ssend_sem.at[c, k], srecv_sem.at[c, q], row, t * 2 + core)

    def finish(c):
        total = ssum[c, q]
        for t in q_from:
            arrived(srecv.at[c, t], srecv_sem.at[c, t])
            total = total + srecv[c, t].astype(jnp.float32)
        part = jnp.dot(total.astype(jnp.bfloat16), wfull[c * fc:(c + 1) * fc, :],
                       preferred_element_type=jnp.float32)
        if c == 0:
            acc[...] = part
        elif c < CHUNKS - 1:
            acc[...] += part
        else:
            out_ref[...] = jnp.maximum(acc[...] + part, 0.0).astype(out_ref.dtype)

    for step in range(CHUNKS + LATE + 2):
        if step + AHEAD < CHUNKS:
            own(step + AHEAD)
        if step < CHUNKS:
            w_own(step)
            forward(step)
        if step == WFWD:
            w_forward()
        if 0 <= step - LATE < CHUNKS:
            aggregate(step - LATE)
        if 0 <= step - LATE - 1 < CHUNKS:
            pair_sum(step - LATE - 1)
        if step == max(WFWD, LATE + 2):
            w_arrive()
        if 0 <= step - LATE - 2 < CHUNKS:
            finish(step - LATE - 2)
    for copy, present in sends:
        if present is None:
            copy.wait_send()
        else:
            pl.when(present)(copy.wait_send)


def solution(mesh):
    rows_n, cols_n = mesh.shape["row"], mesh.shape["col"]
    x_n = 1 << ((rows_n.bit_length() - 1) // 2)
    z_n = rows_n // x_n
    q_n = cols_n // 2

    def body(features, weight, tile_values, block_cols, tile_counts):
        out_rows, feat = features.shape
        _, _, row_blk, slots, bs, _ = tile_values.shape
        fc = feat // CHUNKS
        wide = weight.shape[1]
        dma = pltpu.SemaphoreType.DMA
        bf16, f32 = jnp.bfloat16, jnp.float32
        flops = 2 * row_blk * bs * rows_n * bs * feat + 2 * out_rows * feat * wide
        return pl.pallas_call(
            functools.partial(kernel, rows_n, cols_n, x_n),
            out_shape=jax.ShapeDtypeStruct((out_rows, wide), bf16),
            in_specs=[pl.BlockSpec(memory_space=pltpu.SMEM)] * 2 + [pl.BlockSpec(memory_space=pl.ANY)] * 3,
            out_specs=pl.BlockSpec(memory_space=pltpu.VMEM),
            scratch_shapes=[
                pltpu.VMEM((CHUNKS, rows_n, out_rows, fc), bf16),
                pltpu.VMEM((feat, wide), bf16),
                pltpu.VMEM((row_blk, slots, bs, bs), bf16),
                pltpu.VMEM((2, q_n, out_rows, rows_n * bs), bf16),
                pltpu.VMEM((CHUNKS, q_n, out_rows, fc), bf16),
                pltpu.VMEM((CHUNKS, q_n, out_rows, fc), bf16),
                pltpu.VMEM((CHUNKS, q_n, out_rows, fc), f32),
                pltpu.VMEM((CHUNKS, q_n, out_rows, fc), bf16),
                pltpu.VMEM((CHUNKS, q_n, out_rows, fc), bf16),
                pltpu.VMEM((out_rows, wide), f32),
                dma((2 + CHUNKS,)),
                dma((CHUNKS, 2 * z_n)),
                dma((CHUNKS, 2 * z_n, max(1, x_n - 1))),
                dma((CHUNKS, rows_n)),
                dma((CHUNKS, max(1, q_n - 1))),
                dma((q_n,)),
                dma((cols_n,)),
                dma((CHUNKS,)),
                dma((CHUNKS,)),
                dma((CHUNKS, max(1, q_n - 1))),
                dma((CHUNKS, q_n)),
            ],
            compiler_params=pltpu.CompilerParams(
                collective_id=0, has_side_effects=True, vmem_limit_bytes=63 * 1024 * 1024),
            cost_estimate=pl.CostEstimate(flops=flops, bytes_accessed=4 * 1024 * 1024, transcendentals=0),
        )(block_cols, tile_counts, features, weight, tile_values)

    in_specs = (
        P(("col", "row"), None),
        P("col", None),
        P("row", "col", None, None, None, None),
        P("row", "col", None, None),
        P("row", "col", None),
    )
    return jax.shard_map(body, mesh=mesh, in_specs=in_specs, out_specs=P(("row", "col"), None), check_vma=False)
```
